512 devices in a mesh: ctx: 16 (over y_lo, x), ch: 32 (over z, y_hi, core).
Axes of the slice: x: 4, y: 8 (y_hi: 2, y_lo: 4; y = y_hi * 4 + y_lo), z: 8, core: 2. Of those that a mesh axis runs over, the one named last changes fastest.
Arguments:
- conv_input: bfloat16 [4096, 8192], P('ctx', 'ch'), may hold values from -6 to 6
- gate: bfloat16 [4096, 8192], P('ctx', 'ch'), may hold values from -6 to 6
- out_grad: bfloat16 [4096, 8192], P('ctx', 'ch'), may hold values from -6 to 6
- out_weight: bfloat16 [8192, 8192], P('ch'), may hold values from -0.0625 to 0.0625
- filter_taps: bfloat16 [4096, 8192], P('ctx', 'ch'), may hold values from -0.09375 to 0.09375
Outputs:
- input_grad: float32 [4096, 8192], P('ctx', 'ch')
- filter_grad: float32 [4096, 8192], P('ctx', 'ch')
The draws below stay inside these ranges and needn't reach their ends.
All inputs are finite; a program needn't handle non-finite values.
Results may differ from the reference program's by a relative error of at most 0.0029.
Values may be sent and summed in bfloat16 or wider, within the bound.
No kernel may reach another device: no remote copies, remote signals or barrier semaphores. Data moves between devices by JAX's collectives and lax.ppermute only.
A program may use at most 128 MiB of HBM per device.

```python
import jax
import jax.numpy as jnp
from jax import lax

WIDTH = 8192
TOKENS = 4096


def block_scale(stream_key, extent, pieces, smallest, top_value):
    loudness, own = 1.0, jax.random.fold_in(stream_key, 6)
    for dim, shards_of in pieces:
        draws = jnp.exp(jax.random.uniform(jax.random.fold_in(own, dim), (shards_of,), jnp.float32, smallest / len(pieces), top_value / len(pieces)))
        loudness = loudness * jnp.repeat(draws, extent[dim] // shards_of).reshape([-1 if axis == dim else 1 for axis in range(len(extent))])
    return loudness


def bell_draw(stream_key, extent, spread, most, pieces=(), kind=jnp.bfloat16):
    gain = block_scale(stream_key, extent, pieces, -0.22, 0.18) if pieces else 1.0
    entries = jax.random.normal(stream_key, extent, jnp.float32) * spread * gain
    return jnp.minimum(jnp.maximum(entries, -most), most).astype(kind)


def setup_inputs(seed: int = 0) -> dict:
    keys = jax.random.split(jax.random.key(seed), 6)
    return {
        "conv_input": bell_draw(keys[0], (TOKENS, WIDTH), 1.0, 6.0, ((0, 16), (1, 32))),
        "gate": bell_draw(keys[1], (TOKENS, WIDTH), 1.0, 6.0, ((0, 16), (1, 32))),
        "out_grad": bell_draw(keys[2], (TOKENS, WIDTH), 1.0, 6.0, ((0, 16), (1, 32))),
        "out_weight": bell_draw(keys[3], (WIDTH, WIDTH), WIDTH ** -0.5, 0.0625, ((0, 32),)),
        "filter_taps": bell_draw(keys[4], (TOKENS, WIDTH), TOKENS ** -0.5, 0.09375, ((0, 16), (1, 32))),
    }


def reference(conv_input, gate, out_grad, out_weight, filter_taps):
    pre_gate = jnp.dot(out_grad, out_weight.T, preferred_element_type=jnp.float32)
    rounded = lax.optimization_barrier((gate.astype(jnp.float32) * pre_gate).astype(jnp.bfloat16))
    gated = rounded.astype(jnp.float32)
    length = gated.shape[0]
    period = 2 * length
    gated_f = jnp.fft.rfft(gated, n=period, axis=0)
    taps_f = jnp.fft.rfft(filter_taps.astype(jnp.float32), n=period, axis=0)
    input_f = jnp.fft.rfft(conv_input.astype(jnp.float32), n=period, axis=0)
    input_grad = jnp.fft.irfft(gated_f * jnp.conj(taps_f), n=period, axis=0)[:length]
    filter_grad = jnp.fft.irfft(gated_f * jnp.conj(input_f), n=period, axis=0)[:length]
    filter_grad = filter_grad / jnp.sqrt(jnp.float32(length))
    return (input_grad.astype(jnp.float32), filter_grad.astype(jnp.float32))
```

```python
import functools
import math

import jax
import jax.numpy as jnp
import numpy as np
from jax import lax
from jax.experimental import pallas as pl
from jax.experimental.pallas import tpu as pltpu
from jax.sharding import PartitionSpec as P

BF = jnp.bfloat16
F32 = jnp.float32
VMEM_LIMIT = 48 * 1024 * 1024


def halves(table):
    high = table.astype(jnp.bfloat16)
    return high, (table - high.astype(np.float64)).astype(jnp.bfloat16)


def tables(block):
    angle = np.pi * (2 * np.arange(block) + 1)[None, :] / (2 * block)
    sample = np.arange(2 * block)[:, None]
    forward = np.concatenate([np.cos(sample * angle), np.sin(sample * angle)], axis=1)
    lag = block - np.arange(block)[None, :]
    inverse = np.concatenate([np.cos(lag * angle.T), np.sin(lag * angle.T)], axis=0) / block
    return halves(forward) + halves(inverse)


def dot(a, b):
    return jnp.dot(a, b, preferred_element_type=F32)


def window_kernel(moved_ref, high_ref, low_ref, out_ref):
    blocks, _, lanes, block = moved_ref.shape
    rows = blocks * lanes
    for which in range(2):
        now = moved_ref[:, which].reshape(rows, block)
        before = jnp.concatenate([jnp.zeros((lanes, block), BF), now[: rows - lanes]], axis=0)
        window = jnp.concatenate([before, now], axis=1)
        spectrum = dot(window, high_ref[...]) + dot(window, low_ref[...])
        out_ref[which] = spectrum.reshape(blocks, lanes, 2 * block)


def project_kernel(side_ref, weight_ref, grad_ref, gate_ref, out_ref, total):
    step = pl.program_id(0)
    size = gate_ref.shape[0]

    @pl.when(step == 0)
    def _():
        total[...] = jnp.zeros_like(total)

    side = side_ref[0]
    acc = total[...]
    for core in range(2):
        for far in range(2):
            at = (jnp.where(far == 0, side, 1 - side) * 2 + core) * size
            weight = weight_ref[:, pl.ds(pl.multiple_of(at, size), size)]
            acc += lax.dot_general(
                weight, grad_ref[core, far], (((1,), (1,)), ((), ())), preferred_element_type=F32
            )
    total[...] = acc

    @pl.when(step == pl.num_programs(0) - 1)
    def _():
        out_ref[...] = (gate_ref[...].astype(F32).T * total[...]).astype(BF)


def correlate_kernel(scale, grad_ref, window_ref, high_ref, low_ref, ihigh_ref, ilow_ref, out_ref, spec, cross):
    blocks, lanes, block = grad_ref.shape
    rows = blocks * lanes
    grad = grad_ref[...].reshape(rows, block)
    spec[...] = (dot(grad, high_ref[...]) + dot(grad, low_ref[...])).reshape(blocks, lanes, 2 * block)
    zero = jnp.zeros((lanes, block), F32)
    for first in range(blocks):

        def add(d, totals, first=first):
            re, im = spec[first + d, :, :block], spec[first + d, :, block:]
            out = []
            for which in range(2):
                wre, wim = window_ref[which, d, :, :block], window_ref[which, d, :, block:]
                out.append(totals[2 * which] + (re * wre + im * wim))
                out.append(totals[2 * which + 1] + (re * wim - im * wre))
            return tuple(out)

        totals = (zero,) * 4
        for d in range(blocks - first):
            totals = add(d, totals)
        for which in range(2):
            cross[which, first, :, :block] = totals[2 * which]
            cross[which, first, :, block:] = totals[2 * which + 1]
    for which in range(2):
        full = cross[which].reshape(rows, 2 * block)
        high = full.astype(BF)
        low = (full - high.astype(F32)).astype(BF)
        lags = dot(high, ihigh_ref[...]) + dot(high, ilow_ref[...]) + dot(low, ihigh_ref[...])
        if which == 1:
            lags = lags * scale
        out_ref[:, which] = lags.astype(BF).reshape(blocks, lanes, block)


def finish_kernel(moved_ref, first_ref, second_ref):
    groups, _, lanes, block = moved_ref.shape
    for which, out_ref in enumerate((first_ref, second_ref)):
        out_ref[...] = moved_ref[:, which].reshape(groups * lanes, block).astype(F32).T


def whole(n):
    return [pl.BlockSpec(memory_space=pltpu.VMEM)] * n


def params():
    return pltpu.CompilerParams(vmem_limit_bytes=VMEM_LIMIT)


def shards(conv_input, gate, out_grad, out_weight, filter_taps):
    block, channels = conv_input.shape
    blocks = lax.axis_size("ctx")
    lanes = channels // blocks
    members = lax.axis_size("ch")
    rounds = members // 4
    fhigh, flow, ihigh, ilow = tables(block)

    other = lax.ppermute(out_grad, "ch", [(i, i ^ 2) for i in range(members)])
    near = [[4 * z + 2 * y + c for z in range(rounds) for c in range(2)] for y in range(2)]
    gathered = lax.all_gather(jnp.stack([out_grad, other]), "ch", axis=0, tiled=False, axis_index_groups=near)

    def columns(value):
        return value.T.reshape(blocks, lanes, block)

    sequences = jnp.stack([columns(filter_taps), columns(conv_input)], axis=1)
    sequences = lax.all_to_all(sequences, "ctx", split_axis=0, concat_axis=0, tiled=True)
    windows = pl.pallas_call(
        window_kernel,
        out_shape=jax.ShapeDtypeStruct((2, blocks, lanes, 2 * block), F32),
        in_specs=whole(3),
        out_specs=whole(1)[0],
        compiler_params=params(),
    )(sequences, fhigh, flow)

    side = (lax.axis_index("ch") // 2 % 2).astype(jnp.int32).reshape(1)
    gated = pl.pallas_call(
        project_kernel,
        grid=(rounds,),
        out_shape=jax.ShapeDtypeStruct((channels, block), BF),
        in_specs=[
            pl.BlockSpec(memory_space=pltpu.SMEM),
            pl.BlockSpec((channels, 4 * channels), lambda z: (0, z)),
            pl.BlockSpec((2, 2, block, channels), lambda z: (z, 0, 0, 0)),
            pl.BlockSpec((block, channels), lambda z: (0, 0)),
        ],
        out_specs=pl.BlockSpec((channels, block), lambda z: (0, 0)),
        scratch_shapes=[pltpu.VMEM((channels, block), F32)],
        compiler_params=params(),
    )(side, out_weight, gathered, gate)

    moved = lax.all_to_all(gated.reshape(blocks, lanes, block), "ctx", split_axis=0, concat_axis=0, tiled=True)
    lags = pl.pallas_call(
        functools.partial(correlate_kernel, 1.0 / math.sqrt(blocks * block)),
        out_shape=jax.ShapeDtypeStruct((blocks, 2, lanes, block), BF),
        in_specs=whole(6),
        out_specs=whole(1)[0],
        scratch_shapes=[
            pltpu.VMEM((blocks, lanes, 2 * block), F32),
            pltpu.VMEM((2, blocks, lanes, 2 * block), F32),
        ],
        compiler_params=params(),
    )(moved, windows, fhigh[:block], flow[:block], ihigh, ilow)
    lags = lax.all_to_all(lags, "ctx", split_axis=0, concat_axis=0, tiled=True)
    return pl.pallas_call(
        finish_kernel,
        out_shape=[jax.ShapeDtypeStruct((block, channels), F32)] * 2,
        in_specs=whole(1),
        out_specs=whole(2),
        compiler_params=params(),
    )(lags)


def solution(mesh):
    return jax.shard_map(
        shards,
        mesh=mesh,
        in_specs=(P("ctx", "ch"), P("ctx", "ch"), P("ctx", "ch"), P("ch", None), P("ctx", "ch")),
        out_specs=(P("ctx", "ch"), P("ctx", "ch")),
        check_vma=False,
    )
```

```python
import functools
import math

import jax
import jax.numpy as jnp
import numpy as np
from jax import lax
from jax.experimental import pallas as pl
from jax.experimental.pallas import tpu as pltpu
from jax.sharding import PartitionSpec as P

BF = jnp.bfloat16
F32 = jnp.float32
VMEM_LIMIT = 48 * 1024 * 1024


def halves(table):
    high = table.astype(jnp.bfloat16)
    return high, (table - high.astype(np.float64)).astype(jnp.bfloat16)


def tables(block):
    angle = np.pi * (2 * np.arange(block) + 1)[None, :] / (2 * block)
    sample = np.arange(2 * block)[:, None]
    forward = np.concatenate([np.cos(sample * angle), np.sin(sample * angle)], axis=1)
    lag = block - np.arange(block)[None, :]
    inverse = np.concatenate([np.cos(lag * angle.T), np.sin(lag * angle.T)], axis=0) / block
    return halves(forward) + halves(inverse)


def dot(a, b):
    return jnp.dot(a, b, preferred_element_type=F32)


def slabs(ch, sweeps, size):
    z, side, core = ch // 4, ch // 2 % 2, ch % 2
    place = (z + 8 - core) % 8
    pair, turn = place // 2, 2 * (place % 2) - 1
    pairs = (pair, pair + turn, pair - turn, pair + 2 * turn)
    for sweep in sweeps:
        for far in range(2):
            towards = side if far == 0 else 1 - side
            for spot in range(2):
                at = (2 * (pairs[sweep] + 4) + spot + core) % 8
                yield sweep, far, spot, pl.multiple_of((at * 4 + towards * 2 + core) * size, size)


BOTH_LAST = (((1,), (1,)), ((), ()))


def columns_kernel(gate_ref, taps_ref, input_ref, gate_out, send_ref):
    blocks, _, lanes, block = send_ref.shape
    gate_out[...] = gate_ref[...].astype(F32).T.astype(BF)
    for which, ref in enumerate((taps_ref, input_ref)):
        send_ref[:, which] = ref[...].astype(F32).T.astype(BF).reshape(blocks, lanes, block)


def early_kernel(ch_ref, weight_ref, lent_ref, *rest):
    parts, (sum_ref, kept_ref, slab, slab_done, kept_done) = rest[:6], rest[6:]
    size = weight_ref.shape[0]
    first = list(slabs(ch_ref[0], (0, 1, 2), size))
    last = list(slabs(ch_ref[0], (3,), size))
    copies, keeps = [], []
    for which, ref in enumerate((weight_ref, lent_ref)):
        copies.append([])
        for n, (_, _, _, at) in enumerate(first):
            target = slab.at[which, :, pl.ds(n * size, size)]
            copies[which].append(pltpu.make_async_copy(ref.at[:, pl.ds(at, size)], target, slab_done.at[which, n]))
        for n, (_, _, _, at) in enumerate(last):
            target = kept_ref.at[which, :, pl.ds(n * size, size)]
            keeps.append(pltpu.make_async_copy(ref.at[:, pl.ds(at, size)], target, kept_done.at[which, n]))
    for copy in copies[0] + copies[1] + keeps:
        copy.start()
    grads = jnp.concatenate([parts[2 * sweep + far][spot] for sweep, far, spot, _ in first], axis=1)
    for which in range(2):
        for copy in copies[which]:
            copy.wait()
        sum_ref[which] = lax.dot_general(slab[which], grads, BOTH_LAST, preferred_element_type=F32)
    for copy in keeps:
        copy.wait()


def late_kernel(sum_ref, kept_ref, near_ref, far_ref, own_ref, lend_ref):
    grads = jnp.concatenate([near_ref[0], near_ref[1], far_ref[0], far_ref[1]], axis=1)
    for which, ref in enumerate((own_ref, lend_ref)):
        ref[...] = sum_ref[which] + lax.dot_general(kept_ref[which], grads, BOTH_LAST, preferred_element_type=F32)


def gate_kernel(ch_ref, own_ref, swapped_ref, gate_ref, out_ref):
    pre_gate = own_ref[...] + swapped_ref[1 - ch_ref[0] % 2]
    out_ref[...] = (gate_ref[...].astype(F32) * pre_gate).astype(BF)


def window_kernel(moved_ref, high_ref, low_ref, out_ref):
    blocks, _, lanes, block = moved_ref.shape
    rows = blocks * lanes
    for which in range(2):
        now = moved_ref[:, which].reshape(rows, block)
        before = jnp.concatenate([jnp.zeros((lanes, block), BF), now[: rows - lanes]], axis=0)
        window = jnp.concatenate([before, now], axis=1)
        spectrum = dot(window, high_ref[...]) + dot(window, low_ref[...])
        out_ref[which] = spectrum.reshape(blocks, lanes, 2 * block)


def correlate_kernel(scale, grad_ref, window_ref, high_ref, low_ref, ihigh_ref, ilow_ref, out_ref, spec, cross):
    blocks, lanes, block = grad_ref.shape
    rows = blocks * lanes
    grad = grad_ref[...].reshape(rows, block)
    spec[...] = (dot(grad, high_ref[...]) + dot(grad, low_ref[...])).reshape(blocks, lanes, 2 * block)
    zero = jnp.zeros((lanes, block), F32)
    for first in range(blocks):

        def add(d, totals, first=first):
            re, im = spec[first + d, :, :block], spec[first + d, :, block:]
            out = []
            for which in range(2):
                wre, wim = window_ref[which, d, :, :block], window_ref[which, d, :, block:]
                out.append(totals[2 * which] + (re * wre + im * wim))
                out.append(totals[2 * which + 1] + (re * wim - im * wre))
            return tuple(out)

        totals = (zero,) * 4
        for d in range(blocks - first):
            totals = add(d, totals)
        for which in range(2):
            cross[which, first, :, :block] = totals[2 * which]
            cross[which, first, :, block:] = totals[2 * which + 1]
    for which in range(2):
        full = cross[which].reshape(rows, 2 * block)
        high = full.astype(BF)
        low = (full - high.astype(F32)).astype(BF)
        lags = dot(high, ihigh_ref[...]) + dot(high, ilow_ref[...]) + dot(low, ihigh_ref[...])
        if which == 1:
            lags = lags * scale
        out_ref[:, which] = lags.astype(BF).reshape(blocks, lanes, block)


def finish_kernel(moved_ref, first_ref, second_ref):
    groups, _, lanes, block = moved_ref.shape
    for which, out_ref in enumerate((first_ref, second_ref)):
        out_ref[...] = moved_ref[:, which].reshape(groups * lanes, block).astype(F32).T


def whole(n):
    return [pl.BlockSpec(memory_space=pltpu.VMEM)] * n


def params(limit=VMEM_LIMIT):
    return pltpu.CompilerParams(vmem_limit_bytes=limit)


def shards(conv_input, gate, out_grad, out_weight, filter_taps):
    block, channels = conv_input.shape
    blocks = lax.axis_size("ctx")
    lanes = channels // blocks
    members = lax.axis_size("ch")
    fhigh, flow, ihigh, ilow = tables(block)
    ch = lax.axis_index("ch").astype(jnp.int32)
    ch_ref = ch.reshape(1)
    smem = pl.BlockSpec(memory_space=pltpu.SMEM)

    def spot(z, y, c):
        return z % 8 * 4 + y * 2 + c

    def neighbours(step):
        return [
            [spot(2 * k + (c + step) % 2, y, c), spot(2 * k + 1 + (c + step) % 2, y, c)]
            for k in range(4) for y in range(2) for c in range(2)
        ]

    def swap(value, pairs):
        return lax.ppermute(value, "ch", [(a, b) for pair in pairs for a, b in (pair, pair[::-1])])

    cores = [[i, i + 1] for i in range(0, members, 2)]
    far = swap(out_grad, [[i, i + 2] for i in range(0, members, 4)] + [[i + 1, i + 3] for i in range(0, members, 4)])
    near = lax.all_gather(out_grad, "ch", axis=0, tiled=False, axis_index_groups=neighbours(0))
    columns, sequences = pl.pallas_call(
        columns_kernel,
        out_shape=[
            jax.ShapeDtypeStruct((channels, block), BF),
            jax.ShapeDtypeStruct((blocks, 2, lanes, block), BF),
        ],
        in_specs=whole(3),
        out_specs=whole(2),
        compiler_params=params(62 << 20),
    )(gate, filter_taps, conv_input)
    sequences = lax.all_to_all(sequences, "ctx", split_axis=0, concat_axis=0, tiled=True)
    windows = pl.pallas_call(
        window_kernel,
        out_shape=jax.ShapeDtypeStruct((2, blocks, lanes, 2 * block), F32),
        in_specs=whole(3),
        out_specs=whole(1)[0],
        compiler_params=params(),
    )(sequences, fhigh, flow)
    lent = swap(out_weight, cores)
    far, near, lent, columns = lax.optimization_barrier((far, near, lent, columns))
    far = lax.all_gather(far, "ch", axis=0, tiled=False, axis_index_groups=neighbours(0))
    near, far = lax.optimization_barrier((near, far))
    parts = [near, far]
    for step in (1, 2, 3):
        near, far = swap(near, neighbours(step)), swap(far, neighbours(step))
        if step == 2:
            near, windows = lax.optimization_barrier((near, windows))
        parts += [near, far]

    early, kept = pl.pallas_call(
        early_kernel,
        out_shape=[
            jax.ShapeDtypeStruct((2, channels, block), F32),
            jax.ShapeDtypeStruct((2, channels, 4 * channels), BF),
        ],
        in_specs=[smem] + [pl.BlockSpec(memory_space=pl.ANY)] * 2 + whole(6),
        out_specs=whole(2),
        scratch_shapes=[
            pltpu.VMEM((2, channels, 12 * channels), BF),
            pltpu.SemaphoreType.DMA((2, 12)),
            pltpu.SemaphoreType.DMA((2, 4)),
        ],
        compiler_params=params(),
        cost_estimate=pl.CostEstimate(flops=2 * 2 * 3072 * 256 * 256, bytes_accessed=8 << 20, transcendentals=0),
    )(ch_ref, out_weight, lent, *parts[:6])
    own, lend = pl.pallas_call(
        late_kernel,
        out_shape=[jax.ShapeDtypeStruct((channels, block), F32)] * 2,
        in_specs=whole(4),
        out_specs=whole(2),
        compiler_params=params(),
    )(early, kept, *parts[6:])
    swapped = lax.all_gather(lend, "ch", axis=0, tiled=False, axis_index_groups=cores)
    gated = pl.pallas_call(
        gate_kernel,
        out_shape=jax.ShapeDtypeStruct((channels, block), BF),
        in_specs=[smem] + whole(3),
        out_specs=whole(1)[0],
        compiler_params=params(),
    )(ch_ref, own, swapped, columns)

    moved = lax.all_to_all(gated.reshape(blocks, lanes, block), "ctx", split_axis=0, concat_axis=0, tiled=True)
    lags = pl.pallas_call(
        functools.partial(correlate_kernel, 1.0 / math.sqrt(blocks * block)),
        out_shape=jax.ShapeDtypeStruct((blocks, 2, lanes, block), BF),
        in_specs=whole(6),
        out_specs=whole(1)[0],
        scratch_shapes=[
            pltpu.VMEM((blocks, lanes, 2 * block), F32),
            pltpu.VMEM((2, blocks, lanes, 2 * block), F32),
        ],
        compiler_params=params(),
    )(moved, windows, fhigh[:block], flow[:block], ihigh, ilow)
    lags = lax.all_to_all(lags, "ctx", split_axis=0, concat_axis=0, tiled=True)
    return pl.pallas_call(
        finish_kernel,
        out_shape=[jax.ShapeDtypeStruct((block, channels), F32)] * 2,
        in_specs=whole(1),
        out_specs=whole(2),
        compiler_params=params(),
    )(lags)


def solution(mesh):
    return jax.shard_map(
        shards,
        mesh=mesh,
        in_specs=(P("ctx", "ch"), P("ctx", "ch"), P("ctx", "ch"), P("ch", None), P("ctx", "ch")),
        out_specs=(P("ctx", "ch"), P("ctx", "ch")),
        check_vma=False,
    )
```

```python
import functools
import math

import jax
import jax.numpy as jnp
import numpy as np
from jax import lax
from jax.experimental import pallas as pl
from jax.experimental.pallas import tpu as pltpu
from jax.sharding import PartitionSpec as P

BF = jnp.bfloat16
F32 = jnp.float32
VMEM_LIMIT = 48 * 1024 * 1024


def halves(table):
    high = table.astype(jnp.bfloat16)
    return high, (table - high.astype(np.float64)).astype(jnp.bfloat16)


def tables(block):
    angle = np.pi * (2 * np.arange(block) + 1)[None, :] / (2 * block)
    sample = np.arange(block)[:, None]
    forward = np.concatenate([np.cos(sample * angle), np.sin(sample * angle)], axis=1)
    lag = block - np.arange(block)[None, :]
    inverse = np.concatenate([np.cos(lag * angle.T), np.sin(lag * angle.T)], axis=0) / block
    return halves(forward) + halves(inverse)


def dot(a, b):
    return jnp.dot(a, b, preferred_element_type=F32)


def slabs(ch, sweeps, size):
    z, side, core = ch // 4, ch // 2 % 2, ch % 2
    place = (z + 8 - core) % 8
    pair, turn = place // 2, 2 * (place % 2) - 1
    pairs = (pair, pair + turn, pair - turn, pair + 2 * turn)
    for sweep in sweeps:
        for far in range(2):
            towards = side if far == 0 else 1 - side
            for spot in range(2):
                at = (2 * (pairs[sweep] + 4) + spot + core) % 8
                yield sweep, far, spot, pl.multiple_of((at * 4 + towards * 2 + core) * size, size)


BOTH_LAST = (((1,), (1,)), ((), ()))


def columns_kernel(gate_ref, taps_ref, input_ref, gate_out, send_ref):
    blocks, _, lanes, block = send_ref.shape
    gate_out[...] = gate_ref[...].astype(F32).T.astype(BF)
    for which, ref in enumerate((taps_ref, input_ref)):
        send_ref[:, which] = ref[...].astype(F32).T.astype(BF).reshape(blocks, lanes, block)


def early_kernel(ch_ref, weight_ref, lent_ref, *rest):
    parts, (sum_ref, kept_ref, slab, slab_done, kept_done) = rest[:6], rest[6:]
    size = weight_ref.shape[0]
    first = list(slabs(ch_ref[0], (0, 1, 2), size))
    last = list(slabs(ch_ref[0], (3,), size))
    copies, keeps = [], []
    for which, ref in enumerate((weight_ref, lent_ref)):
        copies.append([])
        for n, (_, _, _, at) in enumerate(first):
            target = slab.at[which, :, pl.ds(n * size, size)]
            copies[which].append(pltpu.make_async_copy(ref.at[:, pl.ds(at, size)], target, slab_done.at[which, n]))
        for n, (_, _, _, at) in enumerate(last):
            target = kept_ref.at[which, :, pl.ds(n * size, size)]
            keeps.append(pltpu.make_async_copy(ref.at[:, pl.ds(at, size)], target, kept_done.at[which, n]))
    for copy in copies[0] + copies[1] + keeps:
        copy.start()
    grads = jnp.concatenate([parts[2 * sweep + far][spot] for sweep, far, spot, _ in first], axis=1)
    for which in range(2):
        for copy in copies[which]:
            copy.wait()
        sum_ref[which] = lax.dot_general(slab[which], grads, BOTH_LAST, preferred_element_type=F32)
    for copy in keeps:
        copy.wait()


def late_kernel(sum_ref, kept_ref, near_ref, far_ref, own_ref, lend_ref):
    grads = jnp.concatenate([near_ref[0], near_ref[1], far_ref[0], far_ref[1]], axis=1)
    for which, ref in enumerate((own_ref, lend_ref)):
        ref[...] = sum_ref[which] + lax.dot_general(kept_ref[which], grads, BOTH_LAST, preferred_element_type=F32)


def gate_kernel(ch_ref, own_ref, swapped_ref, gate_ref, out_ref):
    pre_gate = own_ref[...] + swapped_ref[1 - ch_ref[0] % 2]
    out_ref[...] = (gate_ref[...].astype(F32) * pre_gate).astype(BF)


def correlate_kernel(scale, grad_ref, moved_ref, high_ref, low_ref, ihigh_ref, ilow_ref, out_ref, spec, window, cross):
    blocks, lanes, block = grad_ref.shape
    rows = blocks * lanes

    def transform(value):
        value = value.reshape(rows, block)
        return dot(value, high_ref[...]) + dot(value, low_ref[...])

    spec[...] = transform(grad_ref[...]).reshape(blocks, lanes, 2 * block)
    sign = 1.0 - 2.0 * (lax.broadcasted_iota(jnp.int32, (1, block), 1) % 2).astype(F32)
    none = jnp.zeros((lanes, block), F32)
    for which in range(2):
        now = transform(moved_ref[:, which])
        re, im = now[:, :block], now[:, block:]
        before_re = jnp.concatenate([none, re[: rows - lanes]], axis=0)
        before_im = jnp.concatenate([none, im[: rows - lanes]], axis=0)
        window[which, :, :, :block] = (before_re - sign * im).reshape(blocks, lanes, block)
        window[which, :, :, block:] = (before_im + sign * re).reshape(blocks, lanes, block)
    zero = jnp.zeros((lanes, block), F32)
    for first in range(blocks):

        def add(d, totals, first=first):
            re, im = spec[first + d, :, :block], spec[first + d, :, block:]
            out = []
            for which in range(2):
                wre, wim = window[which, d, :, :block], window[which, d, :, block:]
                out.append(totals[2 * which] + (re * wre + im * wim))
                out.append(totals[2 * which + 1] + (re * wim - im * wre))
            return tuple(out)

        totals = (zero,) * 4
        for d in range(blocks - first):
            totals = add(d, totals)
        for which in range(2):
            cross[which, first, :, :block] = totals[2 * which]
            cross[which, first, :, block:] = totals[2 * which + 1]
    for which in range(2):
        full = cross[which].reshape(rows, 2 * block)
        high = full.astype(BF)
        low = (full - high.astype(F32)).astype(BF)
        lags = dot(high, ihigh_ref[...]) + dot(high, ilow_ref[...]) + dot(low, ihigh_ref[...])
        if which == 1:
            lags = lags * scale
        out_ref[:, which] = lags.astype(BF).reshape(blocks, lanes, block)


def finish_kernel(moved_ref, first_ref, second_ref):
    groups, _, lanes, block = moved_ref.shape
    for which, out_ref in enumerate((first_ref, second_ref)):
        out_ref[...] = moved_ref[:, which].reshape(groups * lanes, block).astype(F32).T


def whole(n):
    return [pl.BlockSpec(memory_space=pltpu.VMEM)] * n


def params(limit=VMEM_LIMIT):
    return pltpu.CompilerParams(vmem_limit_bytes=limit)


def shards(conv_input, gate, out_grad, out_weight, filter_taps):
    block, channels = conv_input.shape
    blocks = lax.axis_size("ctx")
    lanes = channels // blocks
    members = lax.axis_size("ch")
    fhigh, flow, ihigh, ilow = tables(block)
    ch = lax.axis_index("ch").astype(jnp.int32)
    ch_ref = ch.reshape(1)
    smem = pl.BlockSpec(memory_space=pltpu.SMEM)

    def spot(z, y, c):
        return z % 8 * 4 + y * 2 + c

    def neighbours(step):
        return [
            [spot(2 * k + (c + step) % 2, y, c), spot(2 * k + 1 + (c + step) % 2, y, c)]
            for k in range(4) for y in range(2) for c in range(2)
        ]

    def swap(value, pairs):
        return lax.ppermute(value, "ch", [(a, b) for pair in pairs for a, b in (pair, pair[::-1])])

    cores = [[i, i + 1] for i in range(0, members, 2)]
    far = swap(out_grad, [[i, i + 2] for i in range(0, members, 4)] + [[i + 1, i + 3] for i in range(0, members, 4)])
    columns, sequences = pl.pallas_call(
        columns_kernel,
        out_shape=[
            jax.ShapeDtypeStruct((channels, block), BF),
            jax.ShapeDtypeStruct((blocks, 2, lanes, block), BF),
        ],
        in_specs=whole(3),
        out_specs=whole(2),
        compiler_params=params(62 << 20),
    )(gate, filter_taps, conv_input)
    local, columns, sequences = lax.optimization_barrier((out_grad, columns, sequences))
    sequences = lax.all_to_all(sequences, "ctx", split_axis=0, concat_axis=0, tiled=True)
    near = lax.all_gather(local, "ch", axis=0, tiled=False, axis_index_groups=neighbours(0))
    lent = swap(out_weight, cores)
    far, _, lent = lax.optimization_barrier((far, near, lent))
    far = lax.all_gather(far, "ch", axis=0, tiled=False, axis_index_groups=neighbours(0))
    parts = [near, far]
    for step in (1, 2, 3):
        near, far = swap(near, neighbours(step)), swap(far, neighbours(step))
        if step == 2:
            near, sequences = lax.optimization_barrier((near, sequences))
        parts += [near, far]

    early, kept = pl.pallas_call(
        early_kernel,
        out_shape=[
            jax.ShapeDtypeStruct((2, channels, block), F32),
            jax.ShapeDtypeStruct((2, channels, 4 * channels), BF),
        ],
        in_specs=[smem] + [pl.BlockSpec(memory_space=pl.ANY)] * 2 + whole(6),
        out_specs=whole(2),
        scratch_shapes=[
            pltpu.VMEM((2, channels, 12 * channels), BF),
            pltpu.SemaphoreType.DMA((2, 12)),
            pltpu.SemaphoreType.DMA((2, 4)),
        ],
        compiler_params=params(),
        cost_estimate=pl.CostEstimate(flops=2 * 2 * 3072 * 256 * 256, bytes_accessed=8 << 20, transcendentals=0),
    )(ch_ref, out_weight, lent, *parts[:6])
    own, lend = pl.pallas_call(
        late_kernel,
        out_shape=[jax.ShapeDtypeStruct((channels, block), F32)] * 2,
        in_specs=whole(4),
        out_specs=whole(2),
        compiler_params=params(),
    )(early, kept, *parts[6:])
    swapped = lax.all_gather(lend, "ch", axis=0, tiled=False, axis_index_groups=cores)
    gated = pl.pallas_call(
        gate_kernel,
        out_shape=jax.ShapeDtypeStruct((channels, block), BF),
        in_specs=[smem] + whole(3),
        out_specs=whole(1)[0],
        compiler_params=params(),
    )(ch_ref, own, swapped, columns)

    moved = lax.all_to_all(gated.reshape(blocks, lanes, block), "ctx", split_axis=0, concat_axis=0, tiled=True)
    lags = pl.pallas_call(
        functools.partial(correlate_kernel, 1.0 / math.sqrt(blocks * block)),
        out_shape=jax.ShapeDtypeStruct((blocks, 2, lanes, block), BF),
        in_specs=whole(6),
        out_specs=whole(1)[0],
        scratch_shapes=[
            pltpu.VMEM((blocks, lanes, 2 * block), F32),
            pltpu.VMEM((2, blocks, lanes, 2 * block), F32),
            pltpu.VMEM((2, blocks, lanes, 2 * block), F32),
        ],
        compiler_params=params(),
    )(moved, sequences, fhigh, flow, ihigh, ilow)
    lags = lax.all_to_all(lags, "ctx", split_axis=0, concat_axis=0, tiled=True)
    return pl.pallas_call(
        finish_kernel,
        out_shape=[jax.ShapeDtypeStruct((block, channels), F32)] * 2,
        in_specs=whole(1),
        out_specs=whole(2),
        compiler_params=params(),
    )(lags)


def solution(mesh):
    return jax.shard_map(
        shards,
        mesh=mesh,
        in_specs=(P("ctx", "ch"), P("ctx", "ch"), P("ctx", "ch"), P("ch", None), P("ctx", "ch")),
        out_specs=(P("ctx", "ch"), P("ctx", "ch")),
        check_vma=False,
    )
```

```python
import functools
import math

import jax
import jax.numpy as jnp
import numpy as np
from jax import lax
from jax.experimental import pallas as pl
from jax.experimental.pallas import tpu as pltpu
from jax.sharding import PartitionSpec as P

BF = jnp.bfloat16
F32 = jnp.float32
VMEM_LIMIT = 48 * 1024 * 1024


def halves(table):
    high = table.astype(jnp.bfloat16)
    return high, (table - high.astype(np.float64)).astype(jnp.bfloat16)


def tables(block):
    angle = np.pi * (2 * np.arange(block) + 1)[None, :] / (2 * block)
    sample = np.arange(block)[:, None]
    forward = np.concatenate([np.cos(sample * angle), np.sin(sample * angle)], axis=1)
    lag = block - np.arange(block)[None, :]
    inverse = np.concatenate([np.cos(lag * angle.T), np.sin(lag * angle.T)], axis=0) / block
    return halves(forward) + halves(inverse)


def dot(a, b):
    return jnp.dot(a, b, preferred_element_type=F32)


def slabs(ch, sweeps, size):
    z, side, core = ch // 4, ch // 2 % 2, ch % 2
    place = (z + 8 - core) % 8
    pair, turn = place // 2, 2 * (place % 2) - 1
    pairs = (pair, pair + turn, pair - turn, pair + 2 * turn)
    for sweep in sweeps:
        for far in range(2):
            towards = side if far == 0 else 1 - side
            for spot in range(2):
                at = (2 * (pairs[sweep] + 4) + spot + core) % 8
                yield sweep, far, spot, pl.multiple_of((at * 4 + towards * 2 + core) * size, size)


BOTH_LAST = (((1,), (1,)), ((), ()))


def columns_kernel(gate_ref, taps_ref, input_ref, gate_out, send_ref):
    blocks, _, lanes, block = send_ref.shape
    gate_out[...] = gate_ref[...].astype(F32).T.astype(BF)
    for which, ref in enumerate((taps_ref, input_ref)):
        send_ref[:, which] = ref[...].astype(F32).T.astype(BF).reshape(blocks, lanes, block)


def early_kernel(ch_ref, weight_ref, lent_ref, *rest):
    parts, (sum_ref, kept_ref, slab, slab_done, kept_done) = rest[:6], rest[6:]
    size = weight_ref.shape[0]
    first = list(slabs(ch_ref[0], (0, 1, 2), size))
    last = list(slabs(ch_ref[0], (3,), size))
    copies, keeps = [], []
    for which, ref in enumerate((weight_ref, lent_ref)):
        copies.append([])
        for n, (_, _, _, at) in enumerate(first):
            target = slab.at[which, :, pl.ds(n * size, size)]
            copies[which].append(pltpu.make_async_copy(ref.at[:, pl.ds(at, size)], target, slab_done.at[which, n]))
        for n, (_, _, _, at) in enumerate(last):
            target = kept_ref.at[which, :, pl.ds(n * size, size)]
            keeps.append(pltpu.make_async_copy(ref.at[:, pl.ds(at, size)], target, kept_done.at[which, n]))
    for copy in copies[0] + copies[1] + keeps:
        copy.start()
    grads = jnp.concatenate([parts[2 * sweep + far][spot] for sweep, far, spot, _ in first], axis=1)
    for which in range(2):
        for copy in copies[which]:
            copy.wait()
        sum_ref[which] = lax.dot_general(slab[which], grads, BOTH_LAST, preferred_element_type=F32)
    for copy in keeps:
        copy.wait()


def late_kernel(sum_ref, kept_ref, near_ref, far_ref, own_ref, lend_ref):
    grads = jnp.concatenate([near_ref[0], near_ref[1], far_ref[0], far_ref[1]], axis=1)
    for which, ref in enumerate((own_ref, lend_ref)):
        ref[...] = sum_ref[which] + lax.dot_general(kept_ref[which], grads, BOTH_LAST, preferred_element_type=F32)


def gate_kernel(ch_ref, own_ref, swapped_ref, gate_ref, out_ref):
    pre_gate = own_ref[...] + swapped_ref[1 - ch_ref[0] % 2]
    out_ref[...] = (gate_ref[...].astype(F32) * pre_gate).astype(BF)


def correlate_kernel(scale, grad_ref, moved_ref, high_ref, low_ref, ihigh_ref, ilow_ref, out_ref, spec, window, cross):
    blocks, lanes, block = grad_ref.shape
    rows = blocks * lanes

    def transform(value):
        value = value.reshape(rows, block)
        return dot(value, high_ref[...]) + dot(value, low_ref[...])

    spec[...] = transform(grad_ref[...]).reshape(blocks, lanes, 2 * block)
    sign = 1.0 - 2.0 * (lax.broadcasted_iota(jnp.int32, (1, block), 1) % 2).astype(F32)
    none = jnp.zeros((lanes, block), F32)
    for which in range(2):
        now = transform(moved_ref[:, which])
        re, im = now[:, :block], now[:, block:]
        before_re = jnp.concatenate([none, re[: rows - lanes]], axis=0)
        before_im = jnp.concatenate([none, im[: rows - lanes]], axis=0)
        window[which, :, :, :block] = (before_re - sign * im).reshape(blocks, lanes, block)
        window[which, :, :, block:] = (before_im + sign * re).reshape(blocks, lanes, block)
    zero = jnp.zeros((lanes, block), F32)
    for first in range(blocks):

        def add(d, totals, first=first):
            re, im = spec[first + d, :, :block], spec[first + d, :, block:]
            out = []
            for which in range(2):
                wre, wim = window[which, d, :, :block], window[which, d, :, block:]
                out.append(totals[2 * which] + (re * wre + im * wim))
                out.append(totals[2 * which + 1] + (re * wim - im * wre))
            return tuple(out)

        totals = (zero,) * 4
        for d in range(blocks - first):
            totals = add(d, totals)
        for which in range(2):
            cross[which, first, :, :block] = totals[2 * which]
            cross[which, first, :, block:] = totals[2 * which + 1]
    for which in range(2):
        full = cross[which].reshape(rows, 2 * block)
        high = full.astype(BF)
        low = (full - high.astype(F32)).astype(BF)
        lags = dot(high, ihigh_ref[...]) + dot(high, ilow_ref[...]) + dot(low, ihigh_ref[...])
        if which == 1:
            lags = lags * scale
        out_ref[:, which] = lags.astype(BF).reshape(blocks, lanes, block)


def finish_kernel(moved_ref, first_ref, second_ref):
    groups, _, lanes, block = moved_ref.shape
    for which, out_ref in enumerate((first_ref, second_ref)):
        out_ref[...] = moved_ref[:, which].reshape(groups * lanes, block).astype(F32).T


def whole(n):
    return [pl.BlockSpec(memory_space=pltpu.VMEM)] * n


def params(limit=VMEM_LIMIT):
    return pltpu.CompilerParams(vmem_limit_bytes=limit)


def shards(conv_input, gate, out_grad, out_weight, filter_taps):
    block, channels = conv_input.shape
    blocks = lax.axis_size("ctx")
    lanes = channels // blocks
    members = lax.axis_size("ch")
    fhigh, flow, ihigh, ilow = tables(block)
    ch = lax.axis_index("ch").astype(jnp.int32)
    ch_ref = ch.reshape(1)
    smem = pl.BlockSpec(memory_space=pltpu.SMEM)

    def spot(z, y, c):
        return z % 8 * 4 + y * 2 + c

    def neighbours(step):
        return [
            [spot(2 * k + (c + step) % 2, y, c), spot(2 * k + 1 + (c + step) % 2, y, c)]
            for k in range(4) for y in range(2) for c in range(2)
        ]

    def swap(value, pairs):
        return lax.ppermute(value, "ch", [(a, b) for pair in pairs for a, b in (pair, pair[::-1])])

    cores = [[i, i + 1] for i in range(0, members, 2)]
    columns, sequences = pl.pallas_call(
        columns_kernel,
        out_shape=[
            jax.ShapeDtypeStruct((channels, block), BF),
            jax.ShapeDtypeStruct((blocks, 2, lanes, block), BF),
        ],
        in_specs=whole(3),
        out_specs=whole(2),
        compiler_params=params(62 << 20),
    )(gate, filter_taps, conv_input)
    sequences = lax.all_to_all(sequences, "ctx", split_axis=0, concat_axis=0, tiled=True)
    near = lax.all_gather(out_grad, "ch", axis=0, tiled=False, axis_index_groups=neighbours(0))
    lent = swap(out_weight, cores)
    sides = [[spot(z, 0, c), spot(z, 1, c)] for z in range(8) for c in range(2)]
    far = swap(near, sides)
    parts = [near, far]
    for step in (1, 2, 3):
        near, far = swap(near, neighbours(step)), swap(far, neighbours(step))
        if step == 1:
            near, sequences = lax.optimization_barrier((near, sequences))
        parts += [near, far]

    early, kept = pl.pallas_call(
        early_kernel,
        out_shape=[
            jax.ShapeDtypeStruct((2, channels, block), F32),
            jax.ShapeDtypeStruct((2, channels, 4 * channels), BF),
        ],
        in_specs=[smem] + [pl.BlockSpec(memory_space=pl.ANY)] * 2 + whole(6),
        out_specs=whole(2),
        scratch_shapes=[
            pltpu.VMEM((2, channels, 12 * channels), BF),
            pltpu.SemaphoreType.DMA((2, 12)),
            pltpu.SemaphoreType.DMA((2, 4)),
        ],
        compiler_params=params(),
        cost_estimate=pl.CostEstimate(flops=2 * 2 * 3072 * 256 * 256, bytes_accessed=8 << 20, transcendentals=0),
    )(ch_ref, out_weight, lent, *parts[:6])
    own, lend = pl.pallas_call(
        late_kernel,
        out_shape=[jax.ShapeDtypeStruct((channels, block), F32)] * 2,
        in_specs=whole(4),
        out_specs=whole(2),
        compiler_params=params(),
    )(early, kept, *parts[6:])
    swapped = lax.all_gather(lend, "ch", axis=0, tiled=False, axis_index_groups=cores)
    gated = pl.pallas_call(
        gate_kernel,
        out_shape=jax.ShapeDtypeStruct((channels, block), BF),
        in_specs=[smem] + whole(3),
        out_specs=whole(1)[0],
        compiler_params=params(),
    )(ch_ref, own, swapped, columns)

    moved = lax.all_to_all(gated.reshape(blocks, lanes, block), "ctx", split_axis=0, concat_axis=0, tiled=True)
    lags = pl.pallas_call(
        functools.partial(correlate_kernel, 1.0 / math.sqrt(blocks * block)),
        out_shape=jax.ShapeDtypeStruct((blocks, 2, lanes, block), BF),
        in_specs=whole(6),
        out_specs=whole(1)[0],
        scratch_shapes=[
            pltpu.VMEM((blocks, lanes, 2 * block), F32),
            pltpu.VMEM((2, blocks, lanes, 2 * block), F32),
            pltpu.VMEM((2, blocks, lanes, 2 * block), F32),
        ],
        compiler_params=params(),
    )(moved, sequences, fhigh, flow, ihigh, ilow)
    lags = lax.all_to_all(lags, "ctx", split_axis=0, concat_axis=0, tiled=True)
    return pl.pallas_call(
        finish_kernel,
        out_shape=[jax.ShapeDtypeStruct((block, channels), F32)] * 2,
        in_specs=whole(1),
        out_specs=whole(2),
        compiler_params=params(),
    )(lags)


def solution(mesh):
    return jax.shard_map(
        shards,
        mesh=mesh,
        in_specs=(P("ctx", "ch"), P("ctx", "ch"), P("ctx", "ch"), P("ch", None), P("ctx", "ch")),
        out_specs=(P("ctx", "ch"), P("ctx", "ch")),
        check_vma=False,
    )
```

```python
import functools
import math

import jax
import jax.numpy as jnp
import numpy as np
from jax import lax
from jax.experimental import pallas as pl
from jax.experimental.pallas import tpu as pltpu
from jax.sharding import PartitionSpec as P

BF = jnp.bfloat16
F32 = jnp.float32
VMEM_LIMIT = 48 * 1024 * 1024


def halves(table):
    high = table.astype(jnp.bfloat16)
    return high, (table - high.astype(np.float64)).astype(jnp.bfloat16)


def tables(block):
    angle = np.pi * (2 * np.arange(block) + 1)[None, :] / (2 * block)
    sample = np.arange(block)[:, None]
    forward = np.concatenate([np.cos(sample * angle), np.sin(sample * angle)], axis=1)
    lag = block - np.arange(block)[None, :]
    inverse = np.concatenate([np.cos(lag * angle.T), np.sin(lag * angle.T)], axis=0) / block
    return halves(forward) + halves(inverse)


def dot(a, b):
    return jnp.dot(a, b, preferred_element_type=F32)


def slabs(ch, sweeps, size):
    z, side, core = ch // 4, ch // 2 % 2, ch % 2
    place = (z + 8 - core) % 8
    pair, turn = place // 2, 2 * (place % 2) - 1
    pairs = (pair, pair + turn, pair - turn, pair + 2 * turn)
    for sweep in sweeps:
        for far in range(2):
            towards = side if far == 0 else 1 - side
            for spot in range(2):
                at = (2 * (pairs[sweep] + 4) + spot + core) % 8
                yield sweep, far, spot, pl.multiple_of((at * 4 + towards * 2 + core) * size, size)


BOTH_LAST = (((1,), (1,)), ((), ()))


def columns_kernel(gate_ref, taps_ref, input_ref, gate_out, send_ref):
    blocks, _, lanes, block = send_ref.shape
    gate_out[...] = gate_ref[...].astype(F32).T.astype(BF)
    for which, ref in enumerate((taps_ref, input_ref)):
        send_ref[:, which] = ref[...].astype(F32).T.astype(BF).reshape(blocks, lanes, block)


def early_kernel(ch_ref, weight_ref, lent_ref, *rest):
    parts, (sum_ref, kept_ref, slab, slab_done, kept_done) = rest[:6], rest[6:]
    size = weight_ref.shape[0]
    first = list(slabs(ch_ref[0], (0, 1, 2), size))
    last = list(slabs(ch_ref[0], (3,), size))
    copies, keeps = [], []
    for which, ref in enumerate((weight_ref, lent_ref)):
        copies.append([])
        for n, (_, _, _, at) in enumerate(first):
            target = slab.at[which, :, pl.ds(n * size, size)]
            copies[which].append(pltpu.make_async_copy(ref.at[:, pl.ds(at, size)], target, slab_done.at[which, n]))
        for n, (_, _, _, at) in enumerate(last):
            target = kept_ref.at[which, :, pl.ds(n * size, size)]
            keeps.append(pltpu.make_async_copy(ref.at[:, pl.ds(at, size)], target, kept_done.at[which, n]))
    for copy in copies[0] + copies[1] + keeps:
        copy.start()
    grads = jnp.concatenate([parts[2 * sweep + far][spot] for sweep, far, spot, _ in first], axis=1)
    for which in range(2):
        for copy in copies[which]:
            copy.wait()
        sum_ref[which] = lax.dot_general(slab[which], grads, BOTH_LAST, preferred_element_type=F32)
    for copy in keeps:
        copy.wait()


def late_kernel(sum_ref, kept_ref, near_ref, far_ref, own_ref, lend_ref):
    grads = jnp.concatenate([near_ref[0], near_ref[1], far_ref[0], far_ref[1]], axis=1)
    for which, ref in enumerate((own_ref, lend_ref)):
        ref[...] = sum_ref[which] + lax.dot_general(kept_ref[which], grads, BOTH_LAST, preferred_element_type=F32)


def gate_kernel(ch_ref, own_ref, swapped_ref, gate_ref, out_ref):
    pre_gate = own_ref[...] + swapped_ref[1 - ch_ref[0] % 2]
    out_ref[...] = (gate_ref[...].astype(F32) * pre_gate).astype(BF)


def correlate_kernel(scale, grad_ref, moved_ref, high_ref, low_ref, ihigh_ref, ilow_ref, out_ref, spec, window, cross):
    blocks, lanes, block = grad_ref.shape
    rows = blocks * lanes

    def transform(value):
        value = value.reshape(rows, block)
        return dot(value, high_ref[...]) + dot(value, low_ref[...])

    spec[...] = transform(grad_ref[...]).reshape(blocks, lanes, 2 * block)
    sign = 1.0 - 2.0 * (lax.broadcasted_iota(jnp.int32, (1, block), 1) % 2).astype(F32)
    none = jnp.zeros((lanes, block), F32)
    for which in range(2):
        now = transform(moved_ref[:, which])
        re, im = now[:, :block], now[:, block:]
        before_re = jnp.concatenate([none, re[: rows - lanes]], axis=0)
        before_im = jnp.concatenate([none, im[: rows - lanes]], axis=0)
        window[which, :, :, :block] = (before_re - sign * im).reshape(blocks, lanes, block)
        window[which, :, :, block:] = (before_im + sign * re).reshape(blocks, lanes, block)
    zero = jnp.zeros((lanes, block), F32)
    for first in range(blocks):

        def add(d, totals, first=first):
            re, im = spec[first + d, :, :block], spec[first + d, :, block:]
            out = []
            for which in range(2):
                wre, wim = window[which, d, :, :block], window[which, d, :, block:]
                out.append(totals[2 * which] + (re * wre + im * wim))
                out.append(totals[2 * which + 1] + (re * wim - im * wre))
            return tuple(out)

        totals = (zero,) * 4
        for d in range(blocks - first):
            totals = add(d, totals)
        for which in range(2):
            cross[which, first, :, :block] = totals[2 * which]
            cross[which, first, :, block:] = totals[2 * which + 1]
    for which in range(2):
        full = cross[which].reshape(rows, 2 * block)
        high = full.astype(BF)
        low = (full - high.astype(F32)).astype(BF)
        lags = dot(high, ihigh_ref[...]) + dot(high, ilow_ref[...]) + dot(low, ihigh_ref[...])
        if which == 1:
            lags = lags * scale
        out_ref[:, which] = lags.astype(BF).reshape(blocks, lanes, block)


def finish_kernel(moved_ref, first_ref, second_ref):
    groups, _, lanes, block = moved_ref.shape
    for which, out_ref in enumerate((first_ref, second_ref)):
        out_ref[...] = moved_ref[:, which].reshape(groups * lanes, block).astype(F32).T


def whole(n):
    return [pl.BlockSpec(memory_space=pltpu.VMEM)] * n


def params(limit=VMEM_LIMIT):
    return pltpu.CompilerParams(vmem_limit_bytes=limit)


def shards(conv_input, gate, out_grad, out_weight, filter_taps):
    block, channels = conv_input.shape
    blocks = lax.axis_size("ctx")
    lanes = channels // blocks
    members = lax.axis_size("ch")
    fhigh, flow, ihigh, ilow = tables(block)
    ch = lax.axis_index("ch").astype(jnp.int32)
    ch_ref = ch.reshape(1)
    smem = pl.BlockSpec(memory_space=pltpu.SMEM)

    def spot(z, y, c):
        return z % 8 * 4 + y * 2 + c

    def neighbours(step):
        return [
            [spot(2 * k + (c + step) % 2, y, c), spot(2 * k + 1 + (c + step) % 2, y, c)]
            for k in range(4) for y in range(2) for c in range(2)
        ]

    def swap(value, pairs):
        return lax.ppermute(value, "ch", [(a, b) for pair in pairs for a, b in (pair, pair[::-1])])

    cores = [[i, i + 1] for i in range(0, members, 2)]
    columns, sequences = pl.pallas_call(
        columns_kernel,
        out_shape=[
            jax.ShapeDtypeStruct((channels, block), BF),
            jax.ShapeDtypeStruct((blocks, 2, lanes, block), BF),
        ],
        in_specs=whole(3),
        out_specs=whole(2),
        compiler_params=params(62 << 20),
    )(gate, filter_taps, conv_input)
    sequences = lax.all_to_all(sequences, "ctx", split_axis=0, concat_axis=0, tiled=True)
    near = lax.all_gather(out_grad, "ch", axis=0, tiled=False, axis_index_groups=neighbours(0))
    lent = swap(out_weight, cores)
    sides = [[spot(z, 0, c), spot(z, 1, c)] for z in range(8) for c in range(2)]
    far = swap(near, sides)
    parts = [near, far]
    for step in (1, 2, 3):
        far = swap(far, neighbours(step))
        near = swap(near, neighbours(step))
        if step == 1:
            near, sequences = lax.optimization_barrier((near, sequences))
        parts += [near, far]

    early, kept = pl.pallas_call(
        early_kernel,
        out_shape=[
            jax.ShapeDtypeStruct((2, channels, block), F32),
            jax.ShapeDtypeStruct((2, channels, 4 * channels), BF),
        ],
        in_specs=[smem] + [pl.BlockSpec(memory_space=pl.ANY)] * 2 + whole(6),
        out_specs=whole(2),
        scratch_shapes=[
            pltpu.VMEM((2, channels, 12 * channels), BF),
            pltpu.SemaphoreType.DMA((2, 12)),
            pltpu.SemaphoreType.DMA((2, 4)),
        ],
        compiler_params=params(),
        cost_estimate=pl.CostEstimate(flops=2 * 2 * 3072 * 256 * 256, bytes_accessed=8 << 20, transcendentals=0),
    )(ch_ref, out_weight, lent, *parts[:6])
    own, lend = pl.pallas_call(
        late_kernel,
        out_shape=[jax.ShapeDtypeStruct((channels, block), F32)] * 2,
        in_specs=whole(4),
        out_specs=whole(2),
        compiler_params=params(),
    )(early, kept, *parts[6:])
    swapped = lax.all_gather(lend, "ch", axis=0, tiled=False, axis_index_groups=cores)
    gated = pl.pallas_call(
        gate_kernel,
        out_shape=jax.ShapeDtypeStruct((channels, block), BF),
        in_specs=[smem] + whole(3),
        out_specs=whole(1)[0],
        compiler_params=params(),
    )(ch_ref, own, swapped, columns)

    moved = lax.all_to_all(gated.reshape(blocks, lanes, block), "ctx", split_axis=0, concat_axis=0, tiled=True)
    lags = pl.pallas_call(
        functools.partial(correlate_kernel, 1.0 / math.sqrt(blocks * block)),
        out_shape=jax.ShapeDtypeStruct((blocks, 2, lanes, block), BF),
        in_specs=whole(6),
        out_specs=whole(1)[0],
        scratch_shapes=[
            pltpu.VMEM((blocks, lanes, 2 * block), F32),
            pltpu.VMEM((2, blocks, lanes, 2 * block), F32),
            pltpu.VMEM((2, blocks, lanes, 2 * block), F32),
        ],
        compiler_params=params(),
    )(moved, sequences, fhigh, flow, ihigh, ilow)
    lags = lax.all_to_all(lags, "ctx", split_axis=0, concat_axis=0, tiled=True)
    return pl.pallas_call(
        finish_kernel,
        out_shape=[jax.ShapeDtypeStruct((block, channels), F32)] * 2,
        in_specs=whole(1),
        out_specs=whole(2),
        compiler_params=params(),
    )(lags)


def solution(mesh):
    return jax.shard_map(
        shards,
        mesh=mesh,
        in_specs=(P("ctx", "ch"), P("ctx", "ch"), P("ctx", "ch"), P("ch", None), P("ctx", "ch")),
        out_specs=(P("ctx", "ch"), P("ctx", "ch")),
        check_vma=False,
    )
```

```python
import functools
import math

import jax
import jax.numpy as jnp
import numpy as np
from jax import lax
from jax.experimental import pallas as pl
from jax.experimental.pallas import tpu as pltpu
from jax.sharding import PartitionSpec as P

BF = jnp.bfloat16
F32 = jnp.float32
VMEM_LIMIT = 48 * 1024 * 1024


def halves(table):
    high = table.astype(jnp.bfloat16)
    return high, (table - high.astype(np.float64)).astype(jnp.bfloat16)


def tables(block):
    angle = np.pi * (2 * np.arange(block) + 1)[None, :] / (2 * block)
    sample = np.arange(block)[:, None]
    forward = np.concatenate([np.cos(sample * angle), np.sin(sample * angle)], axis=1)
    lag = block - np.arange(block)[None, :]
    inverse = np.concatenate([np.cos(lag * angle.T), np.sin(lag * angle.T)], axis=0) / block
    return halves(forward) + halves(inverse)


def dot(a, b):
    return jnp.dot(a, b, preferred_element_type=F32)


def slabs(ch, sweeps, size):
    z, side, core = ch // 4, ch // 2 % 2, ch % 2
    place = (z + 8 - core) % 8
    pair, turn = place // 2, 2 * (place % 2) - 1
    pairs = (pair, pair + turn, pair - turn, pair + 2 * turn)
    for sweep in sweeps:
        for far in range(2):
            towards = side if far == 0 else 1 - side
            for spot in range(2):
                at = (2 * (pairs[sweep] + 4) + spot + core) % 8
                yield sweep, far, spot, pl.multiple_of((at * 4 + towards * 2 + core) * size, size)


BOTH_LAST = (((1,), (1,)), ((), ()))


def columns_kernel(gate_ref, taps_ref, input_ref, gate_out, send_ref):
    blocks, _, lanes, block = send_ref.shape
    gate_out[...] = gate_ref[...].astype(F32).T.astype(BF)
    for which, ref in enumerate((taps_ref, input_ref)):
        send_ref[:, which] = ref[...].astype(F32).T.astype(BF).reshape(blocks, lanes, block)


def early_kernel(ch_ref, weight_ref, lent_ref, *rest):
    parts, (sum_ref, kept_ref, slab, slab_done, kept_done) = rest[:6], rest[6:]
    size = weight_ref.shape[0]
    first = list(slabs(ch_ref[0], (0, 1, 2), size))
    last = list(slabs(ch_ref[0], (3,), size))
    copies, keeps = [], []
    for which, ref in enumerate((weight_ref, lent_ref)):
        copies.append([])
        for n, (_, _, _, at) in enumerate(first):
            target = slab.at[which, :, pl.ds(n * size, size)]
            copies[which].append(pltpu.make_async_copy(ref.at[:, pl.ds(at, size)], target, slab_done.at[which, n]))
        for n, (_, _, _, at) in enumerate(last):
            target = kept_ref.at[which, :, pl.ds(n * size, size)]
            keeps.append(pltpu.make_async_copy(ref.at[:, pl.ds(at, size)], target, kept_done.at[which, n]))
    for copy in copies[0] + copies[1] + keeps:
        copy.start()
    grads = jnp.concatenate([parts[2 * sweep + far][spot] for sweep, far, spot, _ in first], axis=1)
    for which in range(2):
        for copy in copies[which]:
            copy.wait()
        sum_ref[which] = lax.dot_general(slab[which], grads, BOTH_LAST, preferred_element_type=F32)
    for copy in keeps:
        copy.wait()


def late_kernel(sum_ref, kept_ref, near_ref, far_ref, own_ref, lend_ref):
    grads = jnp.concatenate([near_ref[0], near_ref[1], far_ref[0], far_ref[1]], axis=1)
    for which, ref in enumerate((own_ref, lend_ref)):
        ref[...] = sum_ref[which] + lax.dot_general(kept_ref[which], grads, BOTH_LAST, preferred_element_type=F32)


def gate_kernel(ch_ref, own_ref, swapped_ref, gate_ref, out_ref):
    pre_gate = own_ref[...] + swapped_ref[1 - ch_ref[0] % 2]
    out_ref[...] = (gate_ref[...].astype(F32) * pre_gate).astype(BF)


def correlate_kernel(scale, grad_ref, moved_ref, high_ref, low_ref, ihigh_ref, ilow_ref, out_ref, spec, window, cross):
    blocks, lanes, block = grad_ref.shape
    rows = blocks * lanes

    def transform(value):
        value = value.reshape(rows, block)
        return dot(value, high_ref[...]) + dot(value, low_ref[...])

    spec[...] = transform(grad_ref[...]).reshape(blocks, lanes, 2 * block)
    sign = 1.0 - 2.0 * (lax.broadcasted_iota(jnp.int32, (1, block), 1) % 2).astype(F32)
    none = jnp.zeros((lanes, block), F32)
    for which in range(2):
        now = transform(moved_ref[:, which])
        re, im = now[:, :block], now[:, block:]
        before_re = jnp.concatenate([none, re[: rows - lanes]], axis=0)
        before_im = jnp.concatenate([none, im[: rows - lanes]], axis=0)
        window[which, :, :, :block] = (before_re - sign * im).reshape(blocks, lanes, block)
        window[which, :, :, block:] = (before_im + sign * re).reshape(blocks, lanes, block)
    zero = jnp.zeros((lanes, block), F32)
    for first in range(blocks):

        def add(d, totals, first=first):
            re, im = spec[first + d, :, :block], spec[first + d, :, block:]
            out = []
            for which in range(2):
                wre, wim = window[which, d, :, :block], window[which, d, :, block:]
                out.append(totals[2 * which] + (re * wre + im * wim))
                out.append(totals[2 * which + 1] + (re * wim - im * wre))
            return tuple(out)

        totals = (zero,) * 4
        for d in range(blocks - first):
            totals = add(d, totals)
        for which in range(2):
            cross[which, first, :, :block] = totals[2 * which]
            cross[which, first, :, block:] = totals[2 * which + 1]
    full = cross[...].reshape(2 * rows, 2 * block)
    high = full.astype(BF)
    low = (full - high.astype(F32)).astype(BF)
    lags = dot(high, ihigh_ref[...]) + dot(high, ilow_ref[...]) + dot(low, ihigh_ref[...])
    out_ref[:, 0] = lags[:rows].astype(BF).reshape(blocks, lanes, block)
    out_ref[:, 1] = (lags[rows:] * scale).astype(BF).reshape(blocks, lanes, block)


def finish_kernel(moved_ref, first_ref, second_ref):
    groups, _, lanes, block = moved_ref.shape
    for which, out_ref in enumerate((first_ref, second_ref)):
        out_ref[...] = moved_ref[:, which].reshape(groups * lanes, block).astype(F32).T


def whole(n):
    return [pl.BlockSpec(memory_space=pltpu.VMEM)] * n


def params(limit=VMEM_LIMIT):
    return pltpu.CompilerParams(vmem_limit_bytes=limit)


def shards(conv_input, gate, out_grad, out_weight, filter_taps):
    block, channels = conv_input.shape
    blocks = lax.axis_size("ctx")
    lanes = channels // blocks
    members = lax.axis_size("ch")
    fhigh, flow, ihigh, ilow = tables(block)
    ch = lax.axis_index("ch").astype(jnp.int32)
    ch_ref = ch.reshape(1)
    smem = pl.BlockSpec(memory_space=pltpu.SMEM)

    def spot(z, y, c):
        return z % 8 * 4 + y * 2 + c

    def neighbours(step):
        return [
            [spot(2 * k + (c + step) % 2, y, c), spot(2 * k + 1 + (c + step) % 2, y, c)]
            for k in range(4) for y in range(2) for c in range(2)
        ]

    def swap(value, pairs):
        return lax.ppermute(value, "ch", [(a, b) for pair in pairs for a, b in (pair, pair[::-1])])

    cores = [[i, i + 1] for i in range(0, members, 2)]
    columns, sequences = pl.pallas_call(
        columns_kernel,
        out_shape=[
            jax.ShapeDtypeStruct((channels, block), BF),
            jax.ShapeDtypeStruct((blocks, 2, lanes, block), BF),
        ],
        in_specs=whole(3),
        out_specs=whole(2),
        compiler_params=params(62 << 20),
    )(gate, filter_taps, conv_input)
    sequences = lax.all_to_all(sequences, "ctx", split_axis=0, concat_axis=0, tiled=True)
    near = lax.all_gather(out_grad, "ch", axis=0, tiled=False, axis_index_groups=neighbours(0))
    lent = swap(out_weight, cores)
    sides = [[spot(z, 0, c), spot(z, 1, c)] for z in range(8) for c in range(2)]
    far = swap(near, sides)
    parts = [near, far]
    for step in (1, 2, 3):
        near, far = swap(near, neighbours(step)), swap(far, neighbours(step))
        if step == 1:
            near, sequences = lax.optimization_barrier((near, sequences))
        parts += [near, far]

    early, kept = pl.pallas_call(
        early_kernel,
        out_shape=[
            jax.ShapeDtypeStruct((2, channels, block), F32),
            jax.ShapeDtypeStruct((2, channels, 4 * channels), BF),
        ],
        in_specs=[smem] + [pl.BlockSpec(memory_space=pl.ANY)] * 2 + whole(6),
        out_specs=whole(2),
        scratch_shapes=[
            pltpu.VMEM((2, channels, 12 * channels), BF),
            pltpu.SemaphoreType.DMA((2, 12)),
            pltpu.SemaphoreType.DMA((2, 4)),
        ],
        compiler_params=params(),
        cost_estimate=pl.CostEstimate(flops=2 * 2 * 3072 * 256 * 256, bytes_accessed=8 << 20, transcendentals=0),
    )(ch_ref, out_weight, lent, *parts[:6])
    own, lend = pl.pallas_call(
        late_kernel,
        out_shape=[jax.ShapeDtypeStruct((channels, block), F32)] * 2,
        in_specs=whole(4),
        out_specs=whole(2),
        compiler_params=params(),
    )(early, kept, *parts[6:])
    swapped = lax.all_gather(lend, "ch", axis=0, tiled=False, axis_index_groups=cores)
    gated = pl.pallas_call(
        gate_kernel,
        out_shape=jax.ShapeDtypeStruct((channels, block), BF),
        in_specs=[smem] + whole(3),
        out_specs=whole(1)[0],
        compiler_params=params(),
    )(ch_ref, own, swapped, columns)

    moved = lax.all_to_all(gated.reshape(blocks, lanes, block), "ctx", split_axis=0, concat_axis=0, tiled=True)
    lags = pl.pallas_call(
        functools.partial(correlate_kernel, 1.0 / math.sqrt(blocks * block)),
        out_shape=jax.ShapeDtypeStruct((blocks, 2, lanes, block), BF),
        in_specs=whole(6),
        out_specs=whole(1)[0],
        scratch_shapes=[
            pltpu.VMEM((blocks, lanes, 2 * block), F32),
            pltpu.VMEM((2, blocks, lanes, 2 * block), F32),
            pltpu.VMEM((2, blocks, lanes, 2 * block), F32),
        ],
        compiler_params=params(),
    )(moved, sequences, fhigh, flow, ihigh, ilow)
    lags = lax.all_to_all(lags, "ctx", split_axis=0, concat_axis=0, tiled=True)
    return pl.pallas_call(
        finish_kernel,
        out_shape=[jax.ShapeDtypeStruct((block, channels), F32)] * 2,
        in_specs=whole(1),
        out_specs=whole(2),
        compiler_params=params(),
    )(lags)


def solution(mesh):
    return jax.shard_map(
        shards,
        mesh=mesh,
        in_specs=(P("ctx", "ch"), P("ctx", "ch"), P("ctx", "ch"), P("ch", None), P("ctx", "ch")),
        out_specs=(P("ctx", "ch"), P("ctx", "ch")),
        check_vma=False,
    )
```
